128 devices in a mesh: aux: 32 (over z, x, y_lo), pair: 4 (over y_hi, core).
Axes of the slice: x: 4, y: 4 (y_hi: 2, y_lo: 2; y = y_hi * 2 + y_lo), z: 4, core: 2. Of those that a mesh axis runs over, the one named last changes fastest.
Arguments:
- ia_aux: bfloat16 [16384, 24576], P('pair', 'aux'), may hold values from -0.15625 to 0.15625
- occ_block: int32 [4], replicated, may hold values from 0 to 149
- virt_block: int32 [4], replicated, may hold values from 0 to 19
- owners: int32 [2], replicated, may hold values from 0 to 31
- occ_energy: float32 [1200], replicated, may hold values from -2.5 to -0.4
- virt_energy: float32 [10240], replicated, may hold values from 0.2 to 4
Outputs:
- row_energy: float32 [16384], P(('pair', 'aux'))
- mean_energy: float32 [], replicated
The draws below stay inside these ranges and needn't reach their ends.
All inputs are finite; a program needn't handle non-finite values.
Results may differ from the reference program's by a relative error of at most 0.0003.
Values may be sent and summed in bfloat16 or wider, within the bound.
A program may use at most 128 MiB of HBM per device.

```python
import jax
import jax.numpy as jnp
from jax import lax

OB = 8
VB = 512
NOCC = 1200
NVIRT = 10240
NAUX = 24576
ROWS_DEV = 128
STEPS = 2
ROWS = 16384
NBLK = 4
N_AUX = 32


def with_ends(result, key, smallest, largest):
    index_at = [jax.random.randint(jax.random.fold_in(key, axis), (), 0, length) for axis, length in enumerate(result.shape)]
    longest = result.shape.index(max(result.shape))
    next_to = index_at[:longest] + [(index_at[longest] + 1) % result.shape[longest]] + index_at[longest + 1:]
    return result.at[tuple(index_at)].set(smallest).at[tuple(next_to)].set(largest)


def shard_levels(rng, extent, cuts, smallest, top_value):
    loudness, own = 1.0, jax.random.fold_in(rng, 6)
    for position, shards_of in cuts:
        draws = jnp.exp(jax.random.uniform(jax.random.fold_in(own, position), (shards_of,), jnp.float32, smallest / len(cuts), top_value / len(cuts)))
        loudness = loudness * jnp.repeat(draws, extent[position] // shards_of).reshape([-1 if axis == position else 1 for axis in range(len(extent))])
    return loudness


def centred(rng, dims, spread, most, split=(), held_as=jnp.bfloat16):
    loudness = shard_levels(rng, dims, split, -0.22, 0.18) if split else 1.0
    values = jax.random.normal(rng, dims, jnp.float32) * spread * loudness
    return jnp.minimum(jnp.maximum(values, -most), most).astype(held_as)


def setup_inputs(seed: int = 0) -> dict:
    key_of = jax.random.split(jax.random.key(seed), 7)
    return {
        "ia_aux": centred(key_of[0], (ROWS, NAUX), (NAUX // 16) ** -0.5, 0.15625, ((0, 4), (1, 32))),
        "occ_block": with_ends(jax.random.randint(key_of[1], (NBLK,), 0, NOCC // OB), jax.random.fold_in(key_of[1], 1), 0, (NOCC // OB) - 1).astype(jnp.int32),
        "virt_block": with_ends(jax.random.randint(key_of[2], (NBLK,), 0, NVIRT // VB), jax.random.fold_in(key_of[2], 1), 0, (NVIRT // VB) - 1).astype(jnp.int32),
        "owners": jax.random.randint(key_of[3], (STEPS,), 0, N_AUX).astype(jnp.int32),
        "occ_energy": jnp.clip(jax.random.uniform(key_of[4], (NOCC,), jnp.float32, -2.5, -0.4), -2.5, -0.4),
        "virt_energy": jnp.clip(jax.random.uniform(key_of[5], (NVIRT,), jnp.float32, 0.2, 4.0), 0.2, 4.0),
    }


spin_scale = 1.3


def row_gaps(first_row, row_count, occ_block, virt_block, occ_energy, virt_energy):
    row_index = first_row + jnp.arange(row_count, dtype=jnp.int32)
    per_block = OB * VB
    block_index = row_index // per_block
    within_block = row_index % per_block
    occ_index = (jnp.take(occ_block, block_index) * OB + within_block // VB).astype(jnp.int32)
    virt_index = (jnp.take(virt_block, block_index) * VB + within_block % VB).astype(jnp.int32)
    return jnp.take(virt_energy, virt_index) - jnp.take(occ_energy, occ_index)


def tile_energy(own_rows, partner_rows, own_gaps, partner_gaps):
    intersection = lax.dot_general(own_rows, partner_rows, (((1,), (1,)), ((), ())), preferred_element_type=jnp.float32)
    return jnp.sum(intersection * intersection / (own_gaps[:, None] + partner_gaps[None, :]), axis=1)


def reference(ia_aux, occ_block, virt_block, owners, occ_energy, virt_energy):
    total_rows = ia_aux.shape[0]
    group_count = total_rows // ROWS_DEV
    all_gaps = row_gaps(jnp.int32(0), total_rows, occ_block, virt_block, occ_energy, virt_energy)

    def one_group(group_index):
        pair_index = group_index // N_AUX
        own_first = (group_index * ROWS_DEV).astype(jnp.int32)
        own_rows = lax.dynamic_slice_in_dim(ia_aux, own_first, ROWS_DEV, 0)
        own_gaps = lax.dynamic_slice_in_dim(all_gaps, own_first, ROWS_DEV, 0)
        totals = jnp.zeros((ROWS_DEV,), jnp.float32)
        for turn_index in range(STEPS):
            partner_first = ((pair_index * N_AUX + owners[turn_index]) * ROWS_DEV).astype(jnp.int32)
            partner_rows = lax.dynamic_slice_in_dim(ia_aux, partner_first, ROWS_DEV, 0)
            partner_gaps = lax.dynamic_slice_in_dim(all_gaps, partner_first, ROWS_DEV, 0)
            totals = totals + tile_energy(own_rows, partner_rows, own_gaps, partner_gaps)
        return totals

    group_totals = lax.map(one_group, jnp.arange(group_count, dtype=jnp.int32))
    row_energy = -spin_scale * group_totals.reshape(-1)
    mean_energy = jnp.sum(row_energy) / total_rows
    return row_energy, mean_energy
```

```python
import jax
import jax.numpy as jnp
from jax import lax
from jax.sharding import PartitionSpec as P

OB = 8
VB = 512
STEPS = 2


spin_scale = 1.3


def row_gaps(first_row, row_count, occ_block, virt_block, occ_energy, virt_energy):
    per_block = OB * VB
    block_index = first_row // per_block
    within_block = first_row % per_block
    occ_index = occ_block[block_index] * OB + within_block // VB
    virt_index = virt_block[block_index] * VB + within_block % VB
    return lax.dynamic_slice_in_dim(virt_energy, virt_index, row_count) - occ_energy[occ_index]


def shards(ia_aux, occ_block, virt_block, owners, occ_energy, virt_energy):
    aux_count = lax.axis_size("aux")
    aux_index = lax.axis_index("aux")
    pair_index = lax.axis_index("pair")
    slice_rows = ia_aux.shape[0]
    group_rows = slice_rows // aux_count
    group_base = pair_index * aux_count
    tables = (occ_block, virt_block, occ_energy, virt_energy)
    own_gaps = row_gaps((group_base + aux_index) * group_rows, group_rows, *tables)
    partner_gaps = jnp.concatenate(
        [row_gaps((group_base + owners[t]) * group_rows, group_rows, *tables) for t in range(STEPS)]
    )
    partners = jnp.concatenate(
        [
            lax.dynamic_slice_in_dim(ia_aux, owners[t] * group_rows, group_rows, 0)
            for t in range(STEPS)
        ]
    )
    partial = lax.dot_general(
        ia_aux, partners, (((1,), (1,)), ((), ())), preferred_element_type=jnp.float32
    )
    intersection = lax.psum_scatter(partial, "aux", scatter_dimension=0, tiled=True)
    totals = jnp.sum(
        intersection * intersection / (own_gaps[:, None] + partner_gaps[None, :]), axis=1
    )
    row_energy = -spin_scale * totals
    window_total = lax.psum(jnp.sum(row_energy), ("aux", "pair"))
    mean_energy = window_total / (slice_rows * lax.axis_size("pair"))
    return (row_energy, mean_energy)


def solution(mesh):
    placed = (P("pair", "aux"), P(), P(), P(), P(), P())
    return jax.shard_map(
        shards, mesh=mesh, in_specs=placed, out_specs=(P(("pair", "aux")), P()), check_vma=False
    )
```

```python
import itertools

import jax
import jax.numpy as jnp
from jax import lax
from jax.experimental import pallas as pl
from jax.experimental.pallas import tpu as pltpu
from jax.sharding import PartitionSpec as P

OB = 8
VB = 512
STEPS = 2
GROUP = 128
GROUPS = 32
HALF = GROUP // 2
WIDE = STEPS * GROUP
DEPTH = 768
TOP = 32764.0

MESH = pl.DeviceIdType.MESH
spin_scale = 1.3

FIRST_PEERS = [s for s in itertools.product((0,), range(4), (0,), (0,), range(2)) if any(s)]
SECOND_PEERS = [s for s in itertools.product(range(4), (0,), range(2), range(2), (0,)) if any(s)]


def encode(v, out):
    n = v.shape[0] // 16
    v = v.reshape(n, 16, WIDE)
    top = jnp.max(jnp.abs(v), axis=0)
    power = jnp.ceil(jnp.log2(jnp.maximum(top, 1e-30)))
    q = jnp.round(v * (jnp.exp2(-power) * TOP)[None])
    out[0 : n * 16, :] = q.astype(jnp.int32).astype(jnp.int16).reshape(n * 16, WIDE)
    out[n * 16 : n * 16 + 16, :] = power.astype(jnp.int32).astype(jnp.int16)


def decode(ref):
    n = ref.shape[0] // 16 - 1
    power = ref[n * 16 : n * 16 + 16, :].astype(jnp.int32).astype(jnp.float32)
    q = ref[0 : n * 16, :].astype(jnp.int32).astype(jnp.float32).reshape(n, 16, WIDE)
    return (q * (jnp.exp2(power) * (1.0 / TOP))[None]).reshape(n * 16, WIDE)


def kernel(
    x_hbm, owners, occ_block, virt_block, occ_energy, virt,
    rows_out, mean_out,
    xv, w, keep, own, mid, last, snd1, rcv1, snd2, rcv2, snd3, rcv3, evec, ebuf,
    load_sem, s1s, s1r, s2s, s2r, s3s, s3r, es, er,
):
    aux = lax.axis_index("aux")
    pair = lax.axis_index("pair")
    z, x, y = aux // 8, (aux // 2) % 4, aux % 2
    hi, core = pair // 2, pair % 2

    def device(step, sign=1):
        dz, dx, dy, dh, dc = step
        turn = lambda at, by, n: lax.rem(at + sign * by + 2 * n, n)
        return (
            turn(z, dz, 4) * 8 + turn(x, dx, 4) * 2 + turn(y, dy, 2),
            turn(hi, dh, 2) * 2 + turn(core, dc, 2),
        )

    loads = []
    for i in range(4):
        part = pl.ds(i * 8, 8)
        c = pltpu.make_async_copy(x_hbm.at[part], xv.at[part], load_sem.at[i])
        c.start()
        loads.append(c)

    barrier = pltpu.get_barrier_semaphore()
    peers = FIRST_PEERS + SECOND_PEERS
    for s in peers:
        pl.semaphore_signal(barrier, inc=1, device_id=device(s, -1), device_id_type=MESH)

    def gap_row(u):
        return virt[pl.ds(virt_block[pair] * 4 + u % 4, 1), :] - occ_energy[occ_block[pair] * 8 + u // 4]

    own_gap = jnp.transpose(jnp.broadcast_to(gap_row(aux), (GROUP, GROUP)))
    owner_gap = [gap_row(owners[t]) for t in range(STEPS)]

    for c in loads:
        c.wait()
    for t in range(STEPS):
        w[t * GROUP : (t + 1) * GROUP, :] = xv[owners[t]]

    def partial(h, k):
        parts = []
        for dy in range(2):
            for j in range(4):
                dz, dx = (j, k) if h == 0 else (k, j)
                u = lax.rem(z + dz, 4) * 8 + lax.rem(x + dx, 4) * 2 + lax.rem(y + dy, 2)
                parts.append(xv[u, h * HALF : (h + 1) * HALF, :])
        rows = jnp.concatenate(parts, axis=0)
        return lax.dot_general(rows, w[...], (((1,), (1,)), ((), ())), preferred_element_type=jnp.float32)

    def copy(src, dst, ssem, rsem, step):
        return pltpu.make_async_remote_copy(
            src_ref=src, dst_ref=dst, send_sem=ssem, recv_sem=rsem,
            device_id=device(step), device_id_type=MESH,
        )

    X = ((0, 1, 0, 0, 0), (0, 3, 0, 0, 0))
    Z = ((1, 0, 0, 0, 0), (3, 0, 0, 0, 0))
    WAY = (1, 0, 0, 1, 0, 1)
    started = []

    def send(stage, h, m, v):
        snd, rcv, ssem, rsem = ((snd1, rcv1, s1s, s1r), (snd2, rcv2, s2s, s2r))[stage]
        axis = (X, Z)[(h + stage) % 2]
        i = h * 6 + m
        encode(v, snd.at[i])
        c = copy(snd.at[i], rcv.at[i], ssem.at[i], rsem.at[i], axis[WAY[m]])
        c.start()
        started.append(c)
        return c

    def arrived(stage, h, m, copies):
        copies[(stage, h, m)].wait_recv()
        return decode((rcv1, rcv2)[stage].at[h * 6 + m])

    copies = {}
    n1 = 4 * HALF
    pl.semaphore_wait(barrier, len(peers))

    for h in range(2):
        v = partial(h, 2)
        copies[(0, h, 0)] = send(0, h, 0, v[:n1])
        copies[(0, h, 1)] = send(0, h, 1, v[n1:])
    for h in range(2):
        v = partial(h, 1)
        copies[(0, h, 2)] = send(0, h, 2, v[:n1])
        keep[h, 0] = v[n1:]
        v = partial(h, 3)
        copies[(0, h, 3)] = send(0, h, 3, v[n1:])
        keep[h, 1] = v[:n1]
    for h in range(2):
        own[h] = partial(h, 0)
    for h in range(2):
        copies[(0, h, 4)] = send(0, h, 4, keep[h, 0] + arrived(0, h, 1, copies))
        copies[(0, h, 5)] = send(0, h, 5, keep[h, 1] + arrived(0, h, 0, copies))
    for h in range(2):
        own[h, :n1] += arrived(0, h, 2, copies)
        own[h, n1:] += arrived(0, h, 3, copies)
    for h in range(2):
        own[h, n1:] += arrived(0, h, 4, copies)
        own[h, :n1] += arrived(0, h, 5, copies)

    def block(h, dy, k):
        at = dy * n1 + k * HALF
        return own[h, at : at + HALF]

    for h in range(2):
        copies[(1, h, 0)] = send(1, h, 0, block(h, 0, 2))
        copies[(1, h, 1)] = send(1, h, 1, block(h, 1, 2))
        copies[(1, h, 2)] = send(1, h, 2, block(h, 0, 1))
        copies[(1, h, 3)] = send(1, h, 3, block(h, 1, 3))
    for h in range(2):
        copies[(1, h, 4)] = send(1, h, 4, block(h, 1, 1) + arrived(1, h, 1, copies))
        copies[(1, h, 5)] = send(1, h, 5, block(h, 0, 3) + arrived(1, h, 0, copies))
    for h in range(2):
        mid[h, 1] = block(h, 1, 0) + arrived(1, h, 3, copies)
        mid[h, 0] = block(h, 0, 0) + arrived(1, h, 2, copies)
    cross = []
    for h in range(2):
        encode(mid[h, 1] + arrived(1, h, 4, copies), snd3.at[h])
        c = copy(snd3.at[h], rcv3.at[h], s3s.at[h], s3r.at[h], (0, 0, 1, 0, 0))
        c.start()
        cross.append(c)
    for h in range(2):
        mid[h, 0] += arrived(1, h, 5, copies)
    for h in range(2):
        cross[h].wait_recv()
        whole = mid[h, 0] + decode(rcv3.at[h])
        terms = []
        for t in range(STEPS):
            v = whole[:, t * GROUP : (t + 1) * GROUP]
            gaps = own_gap[h * HALF : (h + 1) * HALF, :] + owner_gap[t]
            terms.append(v * v / gaps)
        last[h * HALF : (h + 1) * HALF, :] = terms[0] + terms[1]
    energy = jnp.sum(jnp.transpose(last[...]), axis=0, keepdims=True) * -spin_scale
    rows_out[...] = energy

    total = energy
    at = 0
    ecopies = []
    for stage, group in enumerate((FIRST_PEERS, SECOND_PEERS)):
        evec[stage] = jnp.broadcast_to(total, (8, GROUP))
        begin = at
        for s in group:
            c = copy(evec.at[stage], ebuf.at[at], es.at[at], er.at[at], s)
            c.start()
            ecopies.append(c)
            at += 1
        for i in range(begin, at):
            ecopies[i].wait_recv()
            total = total + ebuf[i, 0:1]
    mean = jnp.sum(total, axis=1, keepdims=True) * (1.0 / (4 * GROUPS * GROUP))
    mean_out[...] = mean
    for c in started + cross + ecopies:
        c.wait_send()


def shards(ia_aux, occ_block, virt_block, owners, occ_energy, virt_energy):
    smem = pl.BlockSpec(memory_space=pltpu.SMEM)
    vmem = pl.BlockSpec(memory_space=pltpu.VMEM)
    n1, n2 = 4 * HALF + 16, HALF + 16
    peers = len(FIRST_PEERS) + len(SECOND_PEERS)
    dma = lambda n: pltpu.SemaphoreType.DMA((n,))
    row_energy, mean = pl.pallas_call(
        kernel,
        out_shape=(
            jax.ShapeDtypeStruct((1, GROUP), jnp.float32),
            jax.ShapeDtypeStruct((1, 1), jnp.float32),
        ),
        in_specs=[pl.BlockSpec(memory_space=pl.ANY), smem, smem, smem, smem, vmem],
        out_specs=(vmem, vmem),
        scratch_shapes=[
            pltpu.VMEM((GROUPS, GROUP, DEPTH), jnp.bfloat16),
            pltpu.VMEM((WIDE, DEPTH), jnp.bfloat16),
            pltpu.VMEM((2, 2, 4 * HALF, WIDE), jnp.float32),
            pltpu.VMEM((2, 8 * HALF, WIDE), jnp.float32),
            pltpu.VMEM((2, 2, HALF, WIDE), jnp.float32),
            pltpu.VMEM((GROUP, GROUP), jnp.float32),
            pltpu.VMEM((12, n1, WIDE), jnp.int16),
            pltpu.VMEM((12, n1, WIDE), jnp.int16),
            pltpu.VMEM((12, n2, WIDE), jnp.int16),
            pltpu.VMEM((12, n2, WIDE), jnp.int16),
            pltpu.VMEM((2, n2, WIDE), jnp.int16),
            pltpu.VMEM((2, n2, WIDE), jnp.int16),
            pltpu.VMEM((2, 8, GROUP), jnp.float32),
            pltpu.VMEM((peers, 8, GROUP), jnp.float32),
            dma(4), dma(12), dma(12), dma(12), dma(12), dma(2), dma(2), dma(peers), dma(peers),
        ],
        compiler_params=pltpu.CompilerParams(
            collective_id=0, has_side_effects=True, vmem_limit_bytes=56 * 2**20
        ),
    )(
        ia_aux.reshape(GROUPS, GROUP, DEPTH),
        owners,
        occ_block,
        virt_block,
        occ_energy,
        virt_energy.reshape(-1, GROUP),
    )
    return row_energy.reshape(GROUP), mean.reshape(())


def solution(mesh):
    placed = (P("pair", "aux"), P(), P(), P(), P(), P())
    return jax.shard_map(
        shards, mesh=mesh, in_specs=placed, out_specs=(P(("pair", "aux")), P()), check_vma=False
    )
```

```python
import itertools

import jax
import jax.numpy as jnp
from jax import lax
from jax.experimental import pallas as pl
from jax.experimental.pallas import tpu as pltpu
from jax.sharding import PartitionSpec as P

OB = 8
VB = 512
STEPS = 2
GROUP = 128
GROUPS = 32
HALF = GROUP // 2
WIDE = STEPS * GROUP
DEPTH = 768
TOP = 32764.0

MESH = pl.DeviceIdType.MESH
spin_scale = 1.3


def steps(*sizes):
    found = [s for s in itertools.product(*map(range, sizes)) if any(s)]
    return sorted(found, key=lambda s: -sum(min(a, n - a) for a, n in zip(s, (4, 4, 2, 2, 2))))


ENERGY_PEERS = (steps(1, 1, 1, 2, 2), steps(4, 4, 2, 1, 1))
ROW_PEERS = steps(4, 1, 2, 1, 1) + steps(1, 4, 2, 1, 1)
PEERS = ROW_PEERS[:0] + sorted(set(ROW_PEERS) | set(ENERGY_PEERS[0]))


def encode(v, out):
    v = v.reshape(-1, 16, WIDE)
    n = v.shape[0]
    halves = [v[:, :, t * GROUP : (t + 1) * GROUP] for t in range(STEPS)]
    top = jnp.maximum(*[jnp.max(jnp.abs(a), axis=0) for a in halves])
    power = jnp.ceil(jnp.log2(jnp.maximum(top, 1e-30)))
    scale = jnp.exp2(-power) * TOP
    for t, a in enumerate(halves):
        q = jnp.round(a * scale[None]).astype(jnp.int32).astype(jnp.int16)
        out[t * n * 16 : (t + 1) * n * 16, :] = q.reshape(n * 16, GROUP)
    out[STEPS * n * 16 : STEPS * n * 16 + 16, :] = power.astype(jnp.int32).astype(jnp.int16)


def decode(ref):
    rows = (ref.shape[0] - 16) // STEPS
    n = rows // 16
    power = ref[STEPS * rows : STEPS * rows + 16, :].astype(jnp.int32).astype(jnp.float32)
    scale = (jnp.exp2(power) * (1.0 / TOP))[None]
    halves = []
    for t in range(STEPS):
        q = ref[t * rows : (t + 1) * rows, :].astype(jnp.int32).astype(jnp.float32)
        halves.append((q.reshape(n, 16, GROUP) * scale).reshape(rows, GROUP))
    return jnp.concatenate(halves, axis=1)


def coded(rows):
    return STEPS * rows + 16


def loop(n, body):
    def step(i, carry):
        body(i)
        return carry

    lax.fori_loop(0, n, step, 0)


def kernel(
    x_hbm, owners_in, occ_block_in, virt_block_in, occ_energy_in, virt_in,
    rows_out, mean_out,
    owners, occ_block, virt_block, occ_energy, virt, xv, w, part, own_gap, last, evec, ebuf,
    snd1, rcv1, snd2, rcv2,
    load_sem, small_sem, es, er, s1, r1, s2, r2,
):
    aux = lax.axis_index("aux")
    pair = lax.axis_index("pair")
    z, x, y = aux // 8, (aux // 2) % 4, aux % 2
    hi, core = pair // 2, pair % 2

    def device(step, sign=1):
        dz, dx, dy, dh, dc = step
        turn = lambda at, by, n: lax.rem(at + sign * by + 2 * n, n)
        return (
            turn(z, dz, 4) * 8 + turn(x, dx, 4) * 2 + turn(y, dy, 2),
            turn(hi, dh, 2) * 2 + turn(core, dc, 2),
        )

    small = []
    for i, (a, b) in enumerate(
        ((owners_in, owners), (occ_block_in, occ_block), (virt_block_in, virt_block),
         (occ_energy_in, occ_energy), (virt_in, virt))
    ):
        small.append(pltpu.make_async_copy(a, b, small_sem.at[i]))
    loads = []
    for i in range(4):
        rows = pl.ds(i * 8, 8)
        loads.append(pltpu.make_async_copy(x_hbm.at[rows], xv.at[rows], load_sem.at[i]))
    barrier = pltpu.get_barrier_semaphore()
    for c in loads + small:
        c.start()
    for s in PEERS:
        pl.semaphore_signal(barrier, inc=1, device_id=device(s, -1), device_id_type=MESH)
    for c in small:
        c.wait()

    def gap_row(u):
        return virt[pl.ds(virt_block[pair] * 4 + u % 4, 1), :] - occ_energy[occ_block[pair] * 8 + u // 4]

    own_gap[...] = jnp.transpose(jnp.broadcast_to(gap_row(aux), (GROUP, GROUP)))
    owner_gap = [gap_row(owners[t]) for t in range(STEPS)]

    for c in loads:
        c.wait()
    for t in range(STEPS):
        w[t * GROUP : (t + 1) * GROUP, :] = xv[owners[t]].reshape(GROUP, DEPTH)

    def partial(h, k):
        parts = []
        for dy in range(2):
            for j in range(4):
                dz, dx = j * (1 - h) + k * h, k * (1 - h) + j * h
                u = lax.rem(z + dz, 4) * 8 + lax.rem(x + dx, 4) * 2 + lax.rem(y + dy, 2)
                parts.append(xv[u, h])
        rows = jnp.concatenate(parts, axis=0)
        v = lax.dot_general(rows, w[...], (((1,), (1,)), ((), ())), preferred_element_type=jnp.float32)
        part[h, k] = v.reshape(2, 2, 2, HALF, WIDE)

    def copy(src, dst, ssem, rsem, step):
        return pltpu.make_async_remote_copy(
            src_ref=src, dst_ref=dst, send_sem=ssem, recv_sem=rsem,
            device_id=device(step), device_id_type=MESH,
        )

    def post(dy, h, i, v, k):
        encode(v, snd1.at[dy, h, i])
        copy(
            snd1.at[dy, h, i], rcv1.at[dy, h, i], s1.at[dy, h, i], r1.at[dy, h, i],
            (k * h, k * (1 - h), 0, 0, 0),
        ).start()

    def take(dy, h, i):
        ref = rcv1.at[dy, h, i]
        pltpu.make_async_copy(ref, ref, r1.at[dy, h, i]).wait()
        return decode(ref)

    def side(h, k, dy, e):
        return part[h, k, dy, e].reshape(2 * HALF, WIDE)

    def far(dy, h, d):
        post(dy, h, d, side(h, 2, dy, d), 3 - 2 * d)

    def near(dy, h, d):
        post(dy, h, 2 + d, side(h, 1 + 2 * d, dy, d), 1 + 2 * d)

    def relay(dy, h, d):
        post(dy, h, 4 + d, side(h, 1 + 2 * d, dy, 1 - d) + take(dy, h, 1 - d), 1 + 2 * d)

    def gather(dy, h, e):
        v = side(h, 0, dy, e) + take(dy, h, 2 + e) + take(dy, h, 5 - e)
        part[h, 0, dy, e] = v.reshape(2, HALF, WIDE)

    def spread(dy, h, j):
        slot = j if dy else 3 + j
        encode(part[h, 0, dy, j // 2, j % 2], snd2.at[h, slot])
        copy(
            snd2.at[h, slot], rcv2.at[h, slot], s2.at[dy, h], r2.at[dy, h],
            (j * (1 - h), j * h, dy, 0, 0),
        ).start()

    def spread_wait(ref, sem, dy, h):
        here = ref.at[h, pl.ds(0, 4)] if dy else ref.at[h, pl.ds(4, 3)]
        pltpu.make_async_copy(here, here, sem.at[dy, h]).wait()

    def finish(h):
        spread_wait(rcv2, r2, 1, h)
        spread_wait(rcv2, r2, 0, h)
        whole = lax.fori_loop(0, 7, lambda i, v: v + decode(rcv2.at[h, i]), part[h, 0, 0, 0, 0])
        rows = pl.ds(pl.multiple_of(h * HALF, HALF), HALF)
        gaps = own_gap[rows, :]
        terms = []
        for t in range(STEPS):
            v = whole[:, t * GROUP : (t + 1) * GROUP]
            terms.append(v * v / (gaps + owner_gap[t]))
        last[rows, :] = terms[0] + terms[1]

    def close():
        def sent(i):
            dy, h, m = i // 12, (i // 6) % 2, i % 6
            ref = snd1.at[dy, h, m]
            pltpu.make_async_copy(ref, ref, s1.at[dy, h, m]).wait()

        loop(24, sent)
        for h in range(2):
            for dy in range(2):
                spread_wait(snd2, s2, dy, h)

    pairs = lambda f, dy: loop(4, lambda i: f(dy, i // 2, i % 2))

    def begin(h):
        partial(h, 2)
        loop(2, lambda d: far(1, h, d))

    def second(i):
        partial(i // 2, 1 + 2 * (i % 2))
        near(1, i // 2, i % 2)

    pl.semaphore_wait(barrier, len(PEERS))
    loop(2, begin)
    loop(4, second)
    pairs(far, 0)
    loop(2, lambda h: partial(h, 0))
    pairs(relay, 1)
    pairs(near, 0)
    pairs(relay, 0)
    pairs(gather, 1)
    loop(8, lambda i: spread(1, i % 2, lax.rem(i // 2 + 2, 4)))
    pairs(gather, 0)
    loop(6, lambda i: spread(0, i % 2, 1 + lax.rem(i // 2 + 1, 3)))
    loop(2, finish)

    energy = jnp.sum(jnp.transpose(last[...]), axis=0, keepdims=True) * -spin_scale
    rows_out[...] = energy
    total = energy
    at = 0
    for stage, group in enumerate(ENERGY_PEERS):
        evec[stage] = total
        here = ebuf.at[pl.ds(at, len(group))]
        for i, s in enumerate(group):
            copy(evec.at[stage], ebuf.at[at + i], es.at[stage], er.at[stage], s).start()
        pltpu.make_async_copy(here, here, er.at[stage]).wait()
        total = total + jnp.sum(here[...], axis=0)
        at += len(group)
    mean_out[...] = total
    close()
    at = 0
    for stage, group in enumerate(ENERGY_PEERS):
        here = ebuf.at[pl.ds(at, len(group))]
        pltpu.make_async_copy(here, here, es.at[stage]).wait()
        at += len(group)


def tail(rows, total, rows_out, mean_out):
    rows_out[...] = rows[...]
    mean_out[...] = jnp.sum(total[...], axis=1, keepdims=True) * (1.0 / (4 * GROUPS * GROUP))


def shards(ia_aux, occ_block, virt_block, owners, occ_energy, virt_energy):
    vmem = pl.BlockSpec(memory_space=pltpu.VMEM)
    peers = sum(map(len, ENERGY_PEERS))
    stages = len(ENERGY_PEERS)
    dma = lambda *n: pltpu.SemaphoreType.DMA(n)
    row = jax.ShapeDtypeStruct((1, GROUP), jnp.float32)
    row_energy, total = pl.pallas_call(
        kernel,
        out_shape=(row, row),
        in_specs=[pl.BlockSpec(memory_space=pl.ANY)] * 6,
        out_specs=(vmem, vmem),
        scratch_shapes=[
            pltpu.SMEM((STEPS,), jnp.int32),
            pltpu.SMEM(occ_block.shape, jnp.int32),
            pltpu.SMEM(virt_block.shape, jnp.int32),
            pltpu.SMEM(occ_energy.shape, jnp.float32),
            pltpu.VMEM((virt_energy.shape[0] // GROUP, GROUP), jnp.float32),
            pltpu.VMEM((GROUPS, 2, HALF, DEPTH), jnp.bfloat16),
            pltpu.VMEM((WIDE, DEPTH), jnp.bfloat16),
            pltpu.VMEM((2, 4, 2, 2, 2, HALF, WIDE), jnp.float32),
            pltpu.VMEM((GROUP, GROUP), jnp.float32),
            pltpu.VMEM((GROUP, GROUP), jnp.float32),
            pltpu.VMEM((stages, 1, GROUP), jnp.float32),
            pltpu.VMEM((peers, 1, GROUP), jnp.float32),
            pltpu.VMEM((2, 2, 6, coded(2 * HALF), GROUP), jnp.int16),
            pltpu.VMEM((2, 2, 6, coded(2 * HALF), GROUP), jnp.int16),
            pltpu.VMEM((2, 7, coded(HALF), GROUP), jnp.int16),
            pltpu.VMEM((2, 7, coded(HALF), GROUP), jnp.int16),
            dma(4), dma(5), dma(stages), dma(stages),
            dma(2, 2, 6), dma(2, 2, 6), dma(2, 2), dma(2, 2),
        ],
        compiler_params=pltpu.CompilerParams(
            collective_id=0, has_side_effects=True, vmem_limit_bytes=56 * 2**20
        ),
    )(
        ia_aux.reshape(GROUPS, 2, HALF, DEPTH),
        owners,
        occ_block,
        virt_block,
        occ_energy,
        virt_energy.reshape(-1, GROUP),
    )
    row_energy, mean = pl.pallas_call(
        tail, out_shape=(row, jax.ShapeDtypeStruct((1, 1), jnp.float32))
    )(row_energy, total)
    return row_energy.reshape(GROUP), mean.reshape(())


def solution(mesh):
    placed = (P("pair", "aux"), P(), P(), P(), P(), P())
    return jax.shard_map(
        shards, mesh=mesh, in_specs=placed, out_specs=(P(("pair", "aux")), P()), check_vma=False
    )
```

```python
import itertools

import jax
import jax.numpy as jnp
from jax import lax
from jax.experimental import pallas as pl
from jax.experimental.pallas import tpu as pltpu
from jax.sharding import PartitionSpec as P

OB = 8
VB = 512
STEPS = 2
GROUP = 128
GROUPS = 32
HALF = GROUP // 2
WIDE = STEPS * GROUP
DEPTH = 768
TOP = 32764.0

MESH = pl.DeviceIdType.MESH
spin_scale = 1.3
CHIPS = 64


def steps(*sizes):
    return [s for s in itertools.product(*map(range, sizes)) if any(s)]


OTHER_CORE = (0, 0, 0, 0, 1)
OTHER_HALF = (0, 0, 0, 1, 0)
CHIP_PEERS = sorted(
    steps(4, 4, 2, 2, 1), key=lambda s: -sum(min(a, n - a) for a, n in zip(s, (4, 4, 2, 2, 2)))
)
PEERS = sorted(set(steps(4, 1, 2, 1, 1) + steps(1, 4, 2, 1, 1) + [OTHER_CORE, OTHER_HALF]))


def encode(v, out):
    v = v.reshape(-1, 16, WIDE)
    n = v.shape[0]
    halves = [v[:, :, t * GROUP : (t + 1) * GROUP] for t in range(STEPS)]
    top = jnp.maximum(*[jnp.max(jnp.abs(a), axis=0) for a in halves])
    power = jnp.ceil(jnp.log2(jnp.maximum(top, 1e-30)))
    scale = jnp.exp2(-power) * TOP
    for t, a in enumerate(halves):
        q = jnp.round(a * scale[None]).astype(jnp.int32).astype(jnp.int16)
        out[t * n * 16 : (t + 1) * n * 16, :] = q.reshape(n * 16, GROUP)
    out[STEPS * n * 16 : STEPS * n * 16 + 16, :] = power.astype(jnp.int32).astype(jnp.int16)


def decode(ref):
    rows = (ref.shape[0] - 16) // STEPS
    n = rows // 16
    power = ref[STEPS * rows : STEPS * rows + 16, :].astype(jnp.int32).astype(jnp.float32)
    scale = (jnp.exp2(power) * (1.0 / TOP))[None]
    halves = []
    for t in range(STEPS):
        q = ref[t * rows : (t + 1) * rows, :].astype(jnp.int32).astype(jnp.float32)
        halves.append((q.reshape(n, 16, GROUP) * scale).reshape(rows, GROUP))
    return jnp.concatenate(halves, axis=1)


def coded(rows):
    return STEPS * rows + 16


def loop(n, body):
    def step(i, carry):
        body(i)
        return carry

    lax.fori_loop(0, n, step, 0)


def kernel(
    x_hbm, owners_in, occ_block_in, virt_block_in, occ_energy_in, virt_in,
    rows_out, total_out,
    owners, occ_block, virt_block, occ_energy, virt, xv, w, part, own_gap, last, evec, ebuf,
    snd1, rcv1, snd2, rcv2,
    load_sem, small_sem, es, er, s1, r1, s2, r2, hello,
):
    aux = lax.axis_index("aux")
    pair = lax.axis_index("pair")
    z, x, y = aux // 8, (aux // 2) % 4, aux % 2
    hi, core = pair // 2, pair % 2

    def device(step, sign=1):
        dz, dx, dy, dh, dc = step
        turn = lambda at, by, n: lax.rem(at + sign * by + 2 * n, n)
        return (
            turn(z, dz, 4) * 8 + turn(x, dx, 4) * 2 + turn(y, dy, 2),
            turn(hi, dh, 2) * 2 + turn(core, dc, 2),
        )

    small = []
    for i, (a, b) in enumerate(
        ((owners_in, owners), (occ_block_in, occ_block), (virt_block_in, virt_block),
         (occ_energy_in, occ_energy), (virt_in, virt))
    ):
        small.append(pltpu.make_async_copy(a, b, small_sem.at[i]))
    loads = []
    for i in range(4):
        rows = pl.ds(i * 8, 8)
        loads.append(pltpu.make_async_copy(x_hbm.at[rows], xv.at[rows], load_sem.at[i]))
    barrier = pltpu.get_barrier_semaphore()
    for c in loads + small:
        c.start()
    for s in PEERS:
        pl.semaphore_signal(barrier, inc=1, device_id=device(s, -1), device_id_type=MESH)
    for c in small:
        c.wait()

    def gap_row(u):
        return virt[pl.ds(virt_block[pair] * 4 + u % 4, 1), :] - occ_energy[occ_block[pair] * 8 + u // 4]

    own_gap[...] = jnp.transpose(jnp.broadcast_to(gap_row(aux), (GROUP, GROUP)))
    owner_gap = [gap_row(owners[t]) for t in range(STEPS)]

    for c in loads:
        c.wait()
    for t in range(STEPS):
        w[t * GROUP : (t + 1) * GROUP, :] = xv[owners[t]].reshape(GROUP, DEPTH)

    def partial(h, k, dy):
        parts = []
        for j in range(4):
            dz, dx = j * (1 - h) + k * h, k * (1 - h) + j * h
            u = lax.rem(z + dz, 4) * 8 + lax.rem(x + dx, 4) * 2 + lax.rem(y + dy, 2)
            parts.append(xv[u, h])
        rows = jnp.concatenate(parts, axis=0)
        v = lax.dot_general(rows, w[...], (((1,), (1,)), ((), ())), preferred_element_type=jnp.float32)
        part[h, k, dy] = v.reshape(2, 2, HALF, WIDE)

    def copy(src, dst, ssem, rsem, step):
        return pltpu.make_async_remote_copy(
            src_ref=src, dst_ref=dst, send_sem=ssem, recv_sem=rsem,
            device_id=device(step), device_id_type=MESH,
        )

    def post(dy, h, i, v, k):
        encode(v, snd1.at[dy, h, i])
        copy(
            snd1.at[dy, h, i], rcv1.at[dy, h, i], s1.at[dy, h, i], r1.at[dy, h, i],
            (k * h, k * (1 - h), 0, 0, 0),
        ).start()

    def take(dy, h, i):
        ref = rcv1.at[dy, h, i]
        pltpu.make_async_copy(ref, ref, r1.at[dy, h, i]).wait()
        return decode(ref)

    def side(h, k, dy, e):
        return part[h, k, dy, e].reshape(2 * HALF, WIDE)

    def far(dy, h, d):
        post(dy, h, d, side(h, 2, dy, d), 3 - 2 * d)

    def near(dy, h, d):
        post(dy, h, 2 + d, side(h, 1 + 2 * d, dy, d), 1 + 2 * d)

    def relay(dy, h, d):
        post(dy, h, 4 + d, side(h, 1 + 2 * d, dy, 1 - d) + take(dy, h, 1 - d), 1 + 2 * d)

    def gather(dy, h, e):
        v = side(h, 0, dy, e) + take(dy, h, 2 + e) + take(dy, h, 5 - e)
        part[h, 0, dy, e] = v.reshape(2, HALF, WIDE)

    def spread(dy, h, j):
        slot = j if dy else 3 + j
        encode(part[h, 0, dy, j // 2, j % 2], snd2.at[h, slot])
        copy(
            snd2.at[h, slot], rcv2.at[h, slot], s2.at[dy, h], r2.at[dy, h],
            (j * (1 - h), j * h, dy, 0, 0),
        ).start()

    def spread_wait(ref, sem, dy, h):
        here = ref.at[h, pl.ds(0, 4)] if dy else ref.at[h, pl.ds(4, 3)]
        pltpu.make_async_copy(here, here, sem.at[dy, h]).wait()

    def settle(h):
        spread_wait(rcv2, r2, 1, h)
        part[h, 0, 0, 0, 0] = lax.fori_loop(0, 4, lambda i, v: v + decode(rcv2.at[h, i]), part[h, 0, 0, 0, 0])

    def finish(h):
        spread_wait(rcv2, r2, 0, h)
        whole = lax.fori_loop(4, 7, lambda i, v: v + decode(rcv2.at[h, i]), part[h, 0, 0, 0, 0])
        rows = pl.ds(pl.multiple_of(h * HALF, HALF), HALF)
        gaps = own_gap[rows, :]
        terms = []
        for t in range(STEPS):
            v = whole[:, t * GROUP : (t + 1) * GROUP]
            terms.append(v * v / (gaps + owner_gap[t]))
        last[rows, :] = terms[0] + terms[1]

    def close():
        def sent(i):
            dy, h, m = i // 12, (i // 6) % 2, i % 6
            ref = snd1.at[dy, h, m]
            pltpu.make_async_copy(ref, ref, s1.at[dy, h, m]).wait()

        loop(24, sent)
        for h in range(2):
            for dy in range(2):
                spread_wait(snd2, s2, dy, h)

    pairs = lambda f, dy: loop(4, lambda i: f(dy, i // 2, i % 2))

    pl.semaphore_wait(barrier, len(PEERS))
    for k in range(1, 4):
        pl.semaphore_signal(hello.at[0], inc=1, device_id=device((0, k, 0, 0, 0)), device_id_type=MESH)
    def first(h):
        partial(h, 2, 1)
        loop(2, lambda d: far(1, h, d))

    def second(i):
        partial(i // 2, 1 + 2 * (i % 2), 1)
        near(1, i // 2, i % 2)

    def third(h):
        partial(h, 2, 0)
        loop(2, lambda d: far(0, h, d))

    loop(2, first)
    loop(4, second)
    loop(2, third)
    pl.semaphore_wait(hello.at[0], 3)
    pl.semaphore_signal(hello.at[1], inc=1, device_id=device(OTHER_HALF), device_id_type=MESH)
    loop(4, lambda i: partial(i // 2, 1 + 2 * (i % 2), 0))
    pairs(relay, 1)
    pairs(near, 0)
    loop(4, lambda i: partial(i // 2, 0, i % 2))
    pairs(relay, 0)
    pairs(gather, 1)
    loop(8, lambda i: spread(1, i % 2, lax.rem(i // 2 + 2, 4)))
    pairs(gather, 0)
    loop(6, lambda i: spread(0, i % 2, 1 + lax.rem(i // 2 + 1, 3)))
    loop(2, settle)
    loop(2, finish)
    pl.semaphore_wait(hello.at[1], 1)

    total = jnp.sum(last[...], axis=0, keepdims=True) * -spin_scale
    evec[0] = total
    swap = copy(evec.at[0], ebuf.at[CHIPS - 1], es.at[0], er.at[0], (0, 0, 0, 0, 1))
    swap.start()
    rows_out[...] = jnp.sum(jnp.transpose(last[...]), axis=0, keepdims=True) * -spin_scale
    swap.wait_recv()
    total = total + ebuf[CHIPS - 1]
    evec[1] = total

    for i, s in enumerate(CHIP_PEERS):
        copy(evec.at[1], ebuf.at[i], es.at[1], er.at[1], s).start()
    close()
    swap.wait_send()
    here = ebuf.at[pl.ds(0, CHIPS - 1)]
    pltpu.make_async_copy(here, here, es.at[1]).wait()
    pltpu.make_async_copy(here, here, er.at[1]).wait()
    total_out[...] = total + jnp.sum(here[...], axis=0)


def tail(rows, total, rows_out, mean_out):
    rows_out[...] = rows[...]
    mean_out[...] = jnp.sum(total[...], axis=1, keepdims=True) * (1.0 / (4 * GROUPS * GROUP))


def shards(ia_aux, occ_block, virt_block, owners, occ_energy, virt_energy):
    vmem = pl.BlockSpec(memory_space=pltpu.VMEM)
    dma = lambda *n: pltpu.SemaphoreType.DMA(n)
    row = jax.ShapeDtypeStruct((1, GROUP), jnp.float32)
    row_energy, total = pl.pallas_call(
        kernel,
        out_shape=(row, row),
        in_specs=[pl.BlockSpec(memory_space=pl.ANY)] * 6,
        out_specs=(vmem, vmem),
        scratch_shapes=[
            pltpu.SMEM((STEPS,), jnp.int32),
            pltpu.SMEM(occ_block.shape, jnp.int32),
            pltpu.SMEM(virt_block.shape, jnp.int32),
            pltpu.SMEM(occ_energy.shape, jnp.float32),
            pltpu.VMEM((virt_energy.shape[0] // GROUP, GROUP), jnp.float32),
            pltpu.VMEM((GROUPS, 2, HALF, DEPTH), jnp.bfloat16),
            pltpu.VMEM((WIDE, DEPTH), jnp.bfloat16),
            pltpu.VMEM((2, 4, 2, 2, 2, HALF, WIDE), jnp.float32),
            pltpu.VMEM((GROUP, GROUP), jnp.float32),
            pltpu.VMEM((GROUP, GROUP), jnp.float32),
            pltpu.VMEM((2, 1, GROUP), jnp.float32),
            pltpu.VMEM((CHIPS, 1, GROUP), jnp.float32),
            pltpu.VMEM((2, 2, 6, coded(2 * HALF), GROUP), jnp.int16),
            pltpu.VMEM((2, 2, 6, coded(2 * HALF), GROUP), jnp.int16),
            pltpu.VMEM((2, 7, coded(HALF), GROUP), jnp.int16),
            pltpu.VMEM((2, 7, coded(HALF), GROUP), jnp.int16),
            dma(4), dma(5), dma(2), dma(2),
            dma(2, 2, 6), dma(2, 2, 6), dma(2, 2), dma(2, 2), pltpu.SemaphoreType.REGULAR((2,)),
        ],
        compiler_params=pltpu.CompilerParams(
            collective_id=0, has_side_effects=True, vmem_limit_bytes=56 * 2**20
        ),
    )(
        ia_aux.reshape(GROUPS, 2, HALF, DEPTH),
        owners,
        occ_block,
        virt_block,
        occ_energy,
        virt_energy.reshape(-1, GROUP),
    )
    row_energy, mean = pl.pallas_call(
        tail, out_shape=(row, jax.ShapeDtypeStruct((1, 1), jnp.float32))
    )(row_energy, total)
    return row_energy.reshape(GROUP), mean.reshape(())


def solution(mesh):
    placed = (P("pair", "aux"), P(), P(), P(), P(), P())
    return jax.shard_map(
        shards, mesh=mesh, in_specs=placed, out_specs=(P(("pair", "aux")), P()), check_vma=False
    )
```

```python
import itertools

import jax
import jax.numpy as jnp
from jax import lax
from jax.experimental import pallas as pl
from jax.experimental.pallas import tpu as pltpu
from jax.sharding import PartitionSpec as P

OB = 8
VB = 512
STEPS = 2
GROUP = 128
GROUPS = 32
HALF = GROUP // 2
WIDE = STEPS * GROUP
DEPTH = 768
TOP = 32764.0

MESH = pl.DeviceIdType.MESH
spin_scale = 1.3


def steps(*sizes):
    return [s for s in itertools.product(*map(range, sizes)) if any(s)]


OTHER_CORE = (0, 0, 0, 0, 1)
OTHER_HALF = (0, 0, 0, 1, 0)


def hops(s):
    return sum(min(a, n - a) for a, n in zip(s, (4, 4, 2, 2, 2)))


CHIP_PEERS = sorted(steps(4, 4, 2, 2, 1), key=lambda s: -hops(s))
FAR = 0
FAR_CHIPS = [s for s in CHIP_PEERS if hops(s) >= FAR]
NEAR_CHIPS = [s for s in CHIP_PEERS if hops(s) < FAR]
SUMS = 2 * len(FAR_CHIPS) + len(NEAR_CHIPS)
PEERS = sorted(set(steps(4, 1, 2, 1, 1) + steps(1, 4, 2, 1, 1) + [OTHER_CORE, OTHER_HALF]))


def encode(v, out):
    v = v.reshape(-1, 16, WIDE)
    n = v.shape[0]
    halves = [v[:, :, t * GROUP : (t + 1) * GROUP] for t in range(STEPS)]
    top = jnp.maximum(*[jnp.max(jnp.abs(a), axis=0) for a in halves])
    power = jnp.ceil(jnp.log2(jnp.maximum(top, 1e-30)))
    scale = jnp.exp2(-power) * TOP
    for t, a in enumerate(halves):
        q = jnp.round(a * scale[None]).astype(jnp.int32).astype(jnp.int16)
        out[t * n * 16 : (t + 1) * n * 16, :] = q.reshape(n * 16, GROUP)
    out[STEPS * n * 16 : STEPS * n * 16 + 16, :] = power.astype(jnp.int32).astype(jnp.int16)


def decode(ref):
    rows = (ref.shape[0] - 16) // STEPS
    n = rows // 16
    power = ref[STEPS * rows : STEPS * rows + 16, :].astype(jnp.int32).astype(jnp.float32)
    scale = (jnp.exp2(power) * (1.0 / TOP))[None]
    halves = []
    for t in range(STEPS):
        q = ref[t * rows : (t + 1) * rows, :].astype(jnp.int32).astype(jnp.float32)
        halves.append((q.reshape(n, 16, GROUP) * scale).reshape(rows, GROUP))
    return jnp.concatenate(halves, axis=1)


def coded(rows):
    return STEPS * rows + 16


def loop(n, body):
    def step(i, carry):
        body(i)
        return carry

    lax.fori_loop(0, n, step, 0)


def kernel(
    x_hbm, owners_in, occ_block_in, virt_block_in, occ_energy_in, virt_in,
    rows_out, total_out,
    owners, occ_block, virt_block, occ_energy, virt, xv, w, part, own_gap, last, evec, ebuf,
    snd1, rcv1, snd2, rcv2,
    load_sem, small_sem, es, er, s1, r1, s2, r2, hello,
):
    aux = lax.axis_index("aux")
    pair = lax.axis_index("pair")
    z, x, y = aux // 8, (aux // 2) % 4, aux % 2
    hi, core = pair // 2, pair % 2

    zs = [((z + i) % 4) * 8 for i in range(4)]
    xs = [((x + i) % 4) * 2 for i in range(4)]
    ys = [y, 1 - y]
    his = [hi * 2, 2 - hi * 2]
    cores = [core, 1 - core]

    def device(step):
        dz, dx, dy, dh, dc = step
        at = zs[dz] if isinstance(dz, int) else ((z + dz) % 4) * 8
        at = at + (xs[dx] if isinstance(dx, int) else ((x + dx) % 4) * 2)
        return at + (ys[dy] if isinstance(dy, int) else (y + dy) % 2), his[dh] + cores[dc]

    small = []
    for i, (a, b) in enumerate(
        ((owners_in, owners), (occ_block_in, occ_block), (virt_block_in, virt_block),
         (occ_energy_in, occ_energy), (virt_in, virt))
    ):
        small.append(pltpu.make_async_copy(a, b, small_sem.at[i]))
    loads = []
    for i in range(4):
        rows = pl.ds(i * 8, 8)
        loads.append(pltpu.make_async_copy(x_hbm.at[rows], xv.at[rows], load_sem.at[i]))
    barrier = pltpu.get_barrier_semaphore()
    for c in loads + small:
        c.start()
    for s in PEERS:
        pl.semaphore_signal(barrier, inc=1, device_id=device(s), device_id_type=MESH)
    for c in small:
        c.wait()

    def gap_row(u):
        return virt[pl.ds(virt_block[pair] * 4 + u % 4, 1), :] - occ_energy[occ_block[pair] * 8 + u // 4]

    own_gap[...] = jnp.transpose(jnp.broadcast_to(gap_row(aux), (GROUP, GROUP)))
    owner_gap = [gap_row(owners[t]) for t in range(STEPS)]

    for c in loads:
        c.wait()
    for t in range(STEPS):
        w[t * GROUP : (t + 1) * GROUP, :] = xv[owners[t]].reshape(GROUP, DEPTH)

    def partial(h, k, dy):
        parts = []
        for j in range(4):
            dz, dx = j * (1 - h) + k * h, k * (1 - h) + j * h
            u = ((z + dz) % 4) * 8 + ((x + dx) % 4) * 2 + ((y + dy) % 2)
            parts.append(xv[u, h])
        rows = jnp.concatenate(parts, axis=0)
        v = lax.dot_general(rows, w[...], (((1,), (1,)), ((), ())), preferred_element_type=jnp.float32)
        part[h, k, dy] = v.reshape(2, 2, HALF, WIDE)

    def copy(src, dst, ssem, rsem, step):
        return pltpu.make_async_remote_copy(
            src_ref=src, dst_ref=dst, send_sem=ssem, recv_sem=rsem,
            device_id=device(step), device_id_type=MESH,
        )

    def post(dy, h, i, v, k):
        encode(v, snd1.at[dy, h, i])
        copy(
            snd1.at[dy, h, i], rcv1.at[dy, h, i], s1.at[dy, h, i], r1.at[dy, h, i],
            (k * h, k * (1 - h), 0, 0, 0),
        ).start()

    def take(dy, h, i):
        ref = rcv1.at[dy, h, i]
        pltpu.make_async_copy(ref, ref, r1.at[dy, h, i]).wait()
        return decode(ref)

    def side(h, k, dy, e):
        return part[h, k, dy, e].reshape(2 * HALF, WIDE)

    def far(dy, h, d):
        post(dy, h, d, side(h, 2, dy, d), 3 - 2 * d)

    def near(dy, h, d):
        post(dy, h, 2 + d, side(h, 1 + 2 * d, dy, d), 1 + 2 * d)

    def relay(dy, h, d):
        post(dy, h, 4 + d, side(h, 1 + 2 * d, dy, 1 - d) + take(dy, h, 1 - d), 1 + 2 * d)

    def gather(dy, h, e):
        v = side(h, 0, dy, e) + take(dy, h, 2 + e) + take(dy, h, 5 - e)
        part[h, 0, dy, e] = v.reshape(2, HALF, WIDE)

    def spread(dy, h, j):
        slot = j if dy else 3 + j
        encode(part[h, 0, dy, j // 2, j % 2], snd2.at[h, slot])
        copy(
            snd2.at[h, slot], rcv2.at[h, slot], s2.at[dy, h], r2.at[dy, h],
            (j * (1 - h), j * h, dy, 0, 0),
        ).start()

    def spread_wait(ref, sem, dy, h):
        here = ref.at[h, pl.ds(0, 4)] if dy else ref.at[h, pl.ds(4, 3)]
        pltpu.make_async_copy(here, here, sem.at[dy, h]).wait()

    def settle(h):
        spread_wait(rcv2, r2, 1, h)
        part[h, 0, 0, 0, 0] = lax.fori_loop(0, 4, lambda i, v: v + decode(rcv2.at[h, i]), part[h, 0, 0, 0, 0])

    def finish(h):
        spread_wait(rcv2, r2, 0, h)
        whole = lax.fori_loop(4, 7, lambda i, v: v + decode(rcv2.at[h, i]), part[h, 0, 0, 0, 0])
        rows = pl.ds(pl.multiple_of(h * HALF, HALF), HALF)
        gaps = own_gap[rows, :]
        terms = []
        for t in range(STEPS):
            v = whole[:, t * GROUP : (t + 1) * GROUP]
            terms.append(v * v / (gaps + owner_gap[t]))
        last[rows, :] = terms[0] + terms[1]

    def close():
        def sent(i):
            dy, h, m = i // 12, (i // 6) % 2, i % 6
            ref = snd1.at[dy, h, m]
            pltpu.make_async_copy(ref, ref, s1.at[dy, h, m]).wait()

        loop(24, sent)
        for h in range(2):
            for dy in range(2):
                spread_wait(snd2, s2, dy, h)

    pairs = lambda f, dy: loop(4, lambda i: f(dy, i // 2, i % 2))

    pl.semaphore_wait(barrier, len(PEERS))
    for k in range(1, 4):
        pl.semaphore_signal(hello.at[0], inc=1, device_id=device((0, k, 0, 0, 0)), device_id_type=MESH)
    def first(h):
        partial(h, 2, 1)
        loop(2, lambda d: far(1, h, d))

    def second(i):
        partial(i // 2, 1 + 2 * (i % 2), 1)
        near(1, i // 2, i % 2)

    def third(h):
        partial(h, 2, 0)
        loop(2, lambda d: far(0, h, d))

    loop(2, first)
    loop(4, second)
    loop(2, third)
    pl.semaphore_wait(hello.at[0], 3)
    pl.semaphore_signal(hello.at[1], inc=1, device_id=device(OTHER_HALF), device_id_type=MESH)
    loop(4, lambda i: partial(i // 2, 1 + 2 * (i % 2), 0))
    pairs(relay, 1)
    pairs(near, 0)
    loop(4, lambda i: partial(i // 2, 0, i % 2))
    pairs(relay, 0)
    pl.semaphore_wait(hello.at[1], 1)
    pl.semaphore_signal(hello.at[2], inc=1, device_id=device(OTHER_CORE), device_id_type=MESH)
    pairs(gather, 1)
    loop(8, lambda i: spread(1, i % 2, lax.rem(i // 2 + 2, 4)))
    pairs(gather, 0)
    loop(6, lambda i: spread(0, i % 2, 1 + lax.rem(i // 2 + 1, 3)))
    loop(2, settle)
    loop(2, finish)
    pl.semaphore_wait(hello.at[2], 1)

    total = jnp.sum(last[...], axis=0, keepdims=True) * -spin_scale
    evec[0] = total
    swap = copy(evec.at[0], ebuf.at[SUMS], es.at[0], er.at[0], OTHER_CORE)
    swap.start()
    for i, s in enumerate(FAR_CHIPS):
        for c in range(2):
            copy(evec.at[0], ebuf.at[2 * i + c], es.at[1], er.at[1], s[:4] + (c,)).start()
    swap.wait_recv()
    total = total + ebuf[SUMS]
    evec[1] = total
    for i, s in enumerate(NEAR_CHIPS):
        copy(evec.at[1], ebuf.at[2 * len(FAR_CHIPS) + i], es.at[1], er.at[1], s).start()
    rows_out[...] = jnp.sum(jnp.transpose(last[...]), axis=0, keepdims=True) * -spin_scale
    close()
    swap.wait_send()
    here = ebuf.at[pl.ds(0, SUMS)]
    pltpu.make_async_copy(here, here, es.at[1]).wait()
    pltpu.make_async_copy(here, here, er.at[1]).wait()
    total_out[...] = total + jnp.sum(here[...], axis=0)


def tail(rows, total, rows_out, mean_out):
    rows_out[...] = rows[...]
    mean_out[...] = jnp.sum(total[...], axis=1, keepdims=True) * (1.0 / (4 * GROUPS * GROUP))


def shards(ia_aux, occ_block, virt_block, owners, occ_energy, virt_energy):
    vmem = pl.BlockSpec(memory_space=pltpu.VMEM)
    dma = lambda *n: pltpu.SemaphoreType.DMA(n)
    row = jax.ShapeDtypeStruct((1, GROUP), jnp.float32)
    row_energy, total = pl.pallas_call(
        kernel,
        out_shape=(pltpu.VMEM((1, GROUP), jnp.float32), pltpu.VMEM((1, GROUP), jnp.float32)),
        in_specs=[pl.BlockSpec(memory_space=pl.ANY)] * 6,
        out_specs=(vmem, vmem),
        scratch_shapes=[
            pltpu.SMEM((STEPS,), jnp.int32),
            pltpu.SMEM(occ_block.shape, jnp.int32),
            pltpu.SMEM(virt_block.shape, jnp.int32),
            pltpu.SMEM(occ_energy.shape, jnp.float32),
            pltpu.VMEM((virt_energy.shape[0] // GROUP, GROUP), jnp.float32),
            pltpu.VMEM((GROUPS, 2, HALF, DEPTH), jnp.bfloat16),
            pltpu.VMEM((WIDE, DEPTH), jnp.bfloat16),
            pltpu.VMEM((2, 4, 2, 2, 2, HALF, WIDE), jnp.float32),
            pltpu.VMEM((GROUP, GROUP), jnp.float32),
            pltpu.VMEM((GROUP, GROUP), jnp.float32),
            pltpu.VMEM((2, 1, GROUP), jnp.float32),
            pltpu.VMEM((SUMS + 1, 1, GROUP), jnp.float32),
            pltpu.VMEM((2, 2, 6, coded(2 * HALF), GROUP), jnp.int16),
            pltpu.VMEM((2, 2, 6, coded(2 * HALF), GROUP), jnp.int16),
            pltpu.VMEM((2, 7, coded(HALF), GROUP), jnp.int16),
            pltpu.VMEM((2, 7, coded(HALF), GROUP), jnp.int16),
            dma(4), dma(5), dma(2), dma(2),
            dma(2, 2, 6), dma(2, 2, 6), dma(2, 2), dma(2, 2), pltpu.SemaphoreType.REGULAR((3,)),
        ],
        compiler_params=pltpu.CompilerParams(
            collective_id=0, has_side_effects=True, vmem_limit_bytes=56 * 2**20
        ),
    )(
        ia_aux.reshape(GROUPS, 2, HALF, DEPTH),
        owners,
        occ_block,
        virt_block,
        occ_energy,
        virt_energy.reshape(-1, GROUP),
    )
    row_energy, total = (pltpu.with_memory_space_constraint(a, pltpu.VMEM) for a in (row_energy, total))
    row_energy, mean = pl.pallas_call(
        tail, out_shape=(row, jax.ShapeDtypeStruct((1, 1), jnp.float32)), in_specs=[vmem, vmem]
    )(row_energy, total)
    return row_energy.reshape(GROUP), mean.reshape(())


def solution(mesh):
    placed = (P("pair", "aux"), P(), P(), P(), P(), P())
    return jax.shard_map(
        shards, mesh=mesh, in_specs=placed, out_specs=(P(("pair", "aux")), P()), check_vma=False
    )
```

```python
import itertools

import jax
import jax.numpy as jnp
from jax import lax
from jax.experimental import pallas as pl
from jax.experimental.pallas import tpu as pltpu
from jax.sharding import PartitionSpec as P

OB = 8
VB = 512
STEPS = 2
GROUP = 128
GROUPS = 32
HALF = GROUP // 2
WIDE = STEPS * GROUP
DEPTH = 768
TOP = 32764.0

MESH = pl.DeviceIdType.MESH
spin_scale = 1.3


def steps(*sizes):
    return [s for s in itertools.product(*map(range, sizes)) if any(s)]


OTHER_CORE = (0, 0, 0, 0, 1)
OTHER_HALF = (0, 0, 0, 1, 0)


def hops(s):
    return sum(min(a, n - a) for a, n in zip(s, (4, 4, 2, 2, 2)))


ALL_PEERS = sorted(steps(4, 4, 2, 2, 2), key=lambda s: -hops(s))
PEERS = sorted(set(steps(4, 1, 2, 1, 1) + steps(1, 4, 2, 1, 1) + [OTHER_CORE, OTHER_HALF]))


def encode(v, out):
    v = v.reshape(-1, 16, WIDE)
    n = v.shape[0]
    halves = [v[:, :, t * GROUP : (t + 1) * GROUP] for t in range(STEPS)]
    top = jnp.maximum(*[jnp.max(jnp.abs(a), axis=0) for a in halves])
    power = jnp.ceil(jnp.log2(jnp.maximum(top, 1e-30)))
    scale = jnp.exp2(-power) * TOP
    for t, a in enumerate(halves):
        q = jnp.round(a * scale[None]).astype(jnp.int32).astype(jnp.int16)
        out[t * n * 16 : (t + 1) * n * 16, :] = q.reshape(n * 16, GROUP)
    out[STEPS * n * 16 : STEPS * n * 16 + 16, :] = power.astype(jnp.int32).astype(jnp.int16)


def decode(ref):
    rows = (ref.shape[0] - 16) // STEPS
    n = rows // 16
    power = ref[STEPS * rows : STEPS * rows + 16, :].astype(jnp.int32).astype(jnp.float32)
    scale = (jnp.exp2(power) * (1.0 / TOP))[None]
    halves = []
    for t in range(STEPS):
        q = ref[t * rows : (t + 1) * rows, :].astype(jnp.int32).astype(jnp.float32)
        halves.append((q.reshape(n, 16, GROUP) * scale).reshape(rows, GROUP))
    return jnp.concatenate(halves, axis=1)


def coded(rows):
    return STEPS * rows + 16


def loop(n, body):
    def step(i, carry):
        body(i)
        return carry

    lax.fori_loop(0, n, step, 0)


def kernel(
    x_hbm, owners_in, occ_block_in, virt_block_in, occ_energy_in, virt_in,
    rows_out, total_out,
    owners, occ_block, virt_block, occ_energy, virt, xv, w, part, inverse, last, evec, ebuf,
    snd1, rcv1, snd2, rcv2,
    load_sem, small_sem, es, er, s1, r1, s2, r2, hello,
):
    aux = lax.axis_index("aux")
    pair = lax.axis_index("pair")
    z, x, y = aux // 8, (aux // 2) % 4, aux % 2
    hi, core = pair // 2, pair % 2

    zs = [((z + i) % 4) * 8 for i in range(4)]
    xs = [((x + i) % 4) * 2 for i in range(4)]
    ys = [y, 1 - y]
    his = [hi * 2, 2 - hi * 2]
    cores = [core, 1 - core]

    def device(step):
        dz, dx, dy, dh, dc = step
        at = zs[dz] if isinstance(dz, int) else ((z + dz) % 4) * 8
        at = at + (xs[dx] if isinstance(dx, int) else ((x + dx) % 4) * 2)
        return at + (ys[dy] if isinstance(dy, int) else (y + dy) % 2), his[dh] + cores[dc]

    small = []
    for i, (a, b) in enumerate(
        ((owners_in, owners), (occ_block_in, occ_block), (virt_block_in, virt_block),
         (occ_energy_in, occ_energy), (virt_in, virt))
    ):
        small.append(pltpu.make_async_copy(a, b, small_sem.at[i]))
    loads = []
    for i in range(4):
        rows = pl.ds(i * 8, 8)
        loads.append(pltpu.make_async_copy(x_hbm.at[rows], xv.at[rows], load_sem.at[i]))
    barrier = pltpu.get_barrier_semaphore()
    for c in loads + small:
        c.start()
    for s in PEERS:
        pl.semaphore_signal(barrier, inc=1, device_id=device(s), device_id_type=MESH)
    for c in small:
        c.wait()

    def gap_row(u):
        return virt[pl.ds(virt_block[pair] * 4 + u % 4, 1), :] - occ_energy[occ_block[pair] * 8 + u // 4]

    own_gap = jnp.transpose(jnp.broadcast_to(gap_row(aux), (GROUP, GROUP)))
    for t in range(STEPS):
        inverse[t] = 1.0 / (own_gap + gap_row(owners[t]))

    for c in loads:
        c.wait()
    for t in range(STEPS):
        w[t * GROUP : (t + 1) * GROUP, :] = xv[owners[t]].reshape(GROUP, DEPTH)

    def partial(h, k, dy):
        parts = []
        for j in range(4):
            dz, dx = j * (1 - h) + k * h, k * (1 - h) + j * h
            u = ((z + dz) % 4) * 8 + ((x + dx) % 4) * 2 + ((y + dy) % 2)
            parts.append(xv[u, h])
        rows = jnp.concatenate(parts, axis=0)
        v = lax.dot_general(rows, w[...], (((1,), (1,)), ((), ())), preferred_element_type=jnp.float32)
        part[h, k, dy] = v.reshape(2, 2, HALF, WIDE)

    def copy(src, dst, ssem, rsem, step):
        return pltpu.make_async_remote_copy(
            src_ref=src, dst_ref=dst, send_sem=ssem, recv_sem=rsem,
            device_id=device(step), device_id_type=MESH,
        )

    def post(dy, h, i, v, k):
        encode(v, snd1.at[dy, h, i])
        copy(
            snd1.at[dy, h, i], rcv1.at[dy, h, i], s1.at[dy, h, i], r1.at[dy, h, i],
            (k * h, k * (1 - h), 0, 0, 0),
        ).start()

    def take(dy, h, i):
        ref = rcv1.at[dy, h, i]
        pltpu.make_async_copy(ref, ref, r1.at[dy, h, i]).wait()
        return decode(ref)

    def side(h, k, dy, e):
        return part[h, k, dy, e].reshape(2 * HALF, WIDE)

    def far(dy, h, d):
        post(dy, h, d, side(h, 2, dy, d), 3 - 2 * d)

    def near(dy, h, d):
        post(dy, h, 2 + d, side(h, 1 + 2 * d, dy, d), 1 + 2 * d)

    def relay(dy, h, d):
        post(dy, h, 4 + d, side(h, 1 + 2 * d, dy, 1 - d) + take(dy, h, 1 - d), 1 + 2 * d)

    def gather(dy, h, e):
        v = side(h, 0, dy, e) + take(dy, h, 2 + e) + take(dy, h, 5 - e)
        part[h, 0, dy, e] = v.reshape(2, HALF, WIDE)

    def spread(dy, h, j):
        slot = j if dy else 3 + j
        encode(part[h, 0, dy, j // 2, j % 2], snd2.at[h, slot])
        copy(
            snd2.at[h, slot], rcv2.at[h, slot], s2.at[dy, h], r2.at[dy, h],
            (j * (1 - h), j * h, dy, 0, 0),
        ).start()

    def spread_wait(ref, sem, dy, h):
        here = ref.at[h, pl.ds(0, 4)] if dy else ref.at[h, pl.ds(4, 3)]
        pltpu.make_async_copy(here, here, sem.at[dy, h]).wait()

    def settle(h):
        spread_wait(rcv2, r2, 1, h)
        part[h, 0, 0, 0, 0] = part[h, 0, 0, 0, 0] + sum(decode(rcv2.at[h, i]) for i in range(4))

    def finish(h):
        spread_wait(rcv2, r2, 0, h)
        whole = part[h, 0, 0, 0, 0] + sum(decode(rcv2.at[h, i]) for i in range(4, 7))
        rows = pl.ds(h * HALF, HALF)
        terms = []
        for t in range(STEPS):
            v = whole[:, t * GROUP : (t + 1) * GROUP]
            terms.append(v * v * inverse[t, rows, :])
        last[rows, :] = terms[0] + terms[1]

    def close():
        def sent(i):
            dy, h, m = i // 12, (i // 6) % 2, i % 6
            ref = snd1.at[dy, h, m]
            pltpu.make_async_copy(ref, ref, s1.at[dy, h, m]).wait()

        loop(24, sent)
        for h in range(2):
            for dy in range(2):
                spread_wait(snd2, s2, dy, h)

    pairs = lambda f, dy: loop(4, lambda i: f(dy, i // 2, i % 2))

    def first(h):
        partial(h, 2, 1)
        loop(2, lambda d: far(1, h, d))

    def second(i):
        partial(i // 2, 1 + 2 * (i % 2), 1)
        near(1, i // 2, i % 2)

    def third(h):
        partial(h, 2, 0)
        loop(2, lambda d: far(0, h, d))

    partial(0, 2, 1)
    partial(1, 2, 1)
    pl.semaphore_wait(barrier, len(PEERS))
    pairs(far, 1)
    for k in range(1, 4):
        pl.semaphore_signal(hello.at[0], inc=1, device_id=device((0, k, 0, 0, 0)), device_id_type=MESH)
    loop(4, second)
    loop(2, third)
    pl.semaphore_wait(hello.at[0], 3)
    pl.semaphore_signal(hello.at[1], inc=1, device_id=device(OTHER_HALF), device_id_type=MESH)
    loop(4, lambda i: partial(i // 2, 1 + 2 * (i % 2), 0))
    pairs(relay, 1)
    pairs(near, 0)
    loop(4, lambda i: partial(i // 2, 0, i % 2))
    pairs(relay, 0)
    pl.semaphore_wait(hello.at[1], 1)
    pl.semaphore_signal(hello.at[2], inc=1, device_id=device(OTHER_CORE), device_id_type=MESH)
    pairs(gather, 1)
    loop(8, lambda i: spread(1, i % 2, lax.rem(i // 2 + 2, 4)))
    pairs(gather, 0)
    loop(6, lambda i: spread(0, i % 2, 1 + lax.rem(i // 2 + 1, 3)))
    for h in range(2):
        settle(h)
    for h in range(2):
        finish(h)
    pl.semaphore_wait(hello.at[2], 1)

    total = jnp.sum(last[...], axis=0, keepdims=True) * -spin_scale
    evec[...] = total
    for i, s in enumerate(ALL_PEERS):
        copy(evec, ebuf.at[i], es, er, s).start()
    rows_out[...] = jnp.sum(jnp.transpose(last[...]), axis=0, keepdims=True) * -spin_scale
    close()
    pltpu.make_async_copy(ebuf, ebuf, es).wait()
    pltpu.make_async_copy(ebuf, ebuf, er).wait()
    total_out[...] = total + jnp.sum(ebuf[...], axis=0)


def tail(rows, total, rows_out, mean_out):
    rows_out[...] = rows[...]
    mean_out[...] = jnp.sum(total[...], axis=1, keepdims=True) * (1.0 / (4 * GROUPS * GROUP))


def shards(ia_aux, occ_block, virt_block, owners, occ_energy, virt_energy):
    vmem = pl.BlockSpec(memory_space=pltpu.VMEM)
    dma = lambda *n: pltpu.SemaphoreType.DMA(n) if n else pltpu.SemaphoreType.DMA
    row = jax.ShapeDtypeStruct((1, GROUP), jnp.float32)
    row_energy, total = pl.pallas_call(
        kernel,
        out_shape=(pltpu.VMEM((1, GROUP), jnp.float32), pltpu.VMEM((1, GROUP), jnp.float32)),
        in_specs=[pl.BlockSpec(memory_space=pl.ANY)] * 6,
        out_specs=(vmem, vmem),
        scratch_shapes=[
            pltpu.SMEM((STEPS,), jnp.int32),
            pltpu.SMEM(occ_block.shape, jnp.int32),
            pltpu.SMEM(virt_block.shape, jnp.int32),
            pltpu.SMEM(occ_energy.shape, jnp.float32),
            pltpu.VMEM((virt_energy.shape[0] // GROUP, GROUP), jnp.float32),
            pltpu.VMEM((GROUPS, 2, HALF, DEPTH), jnp.bfloat16),
            pltpu.VMEM((WIDE, DEPTH), jnp.bfloat16),
            pltpu.VMEM((2, 4, 2, 2, 2, HALF, WIDE), jnp.float32),
            pltpu.VMEM((STEPS, GROUP, GROUP), jnp.float32),
            pltpu.VMEM((GROUP, GROUP), jnp.float32),
            pltpu.VMEM((1, GROUP), jnp.float32),
            pltpu.VMEM((len(ALL_PEERS), 1, GROUP), jnp.float32),
            pltpu.VMEM((2, 2, 6, coded(2 * HALF), GROUP), jnp.int16),
            pltpu.VMEM((2, 2, 6, coded(2 * HALF), GROUP), jnp.int16),
            pltpu.VMEM((2, 7, coded(HALF), GROUP), jnp.int16),
            pltpu.VMEM((2, 7, coded(HALF), GROUP), jnp.int16),
            dma(4), dma(5), dma(), dma(),
            dma(2, 2, 6), dma(2, 2, 6), dma(2, 2), dma(2, 2), pltpu.SemaphoreType.REGULAR((3,)),
        ],
        compiler_params=pltpu.CompilerParams(
            collective_id=0, has_side_effects=True, vmem_limit_bytes=56 * 2**20
        ),
    )(
        ia_aux.reshape(GROUPS, 2, HALF, DEPTH),
        owners,
        occ_block,
        virt_block,
        occ_energy,
        virt_energy.reshape(-1, GROUP),
    )
    row_energy, total = (pltpu.with_memory_space_constraint(a, pltpu.VMEM) for a in (row_energy, total))
    row_energy, mean = pl.pallas_call(
        tail, out_shape=(row, jax.ShapeDtypeStruct((1, 1), jnp.float32)), in_specs=[vmem, vmem]
    )(row_energy, total)
    return row_energy.reshape(GROUP), mean.reshape(())


def solution(mesh):
    placed = (P("pair", "aux"), P(), P(), P(), P(), P())
    return jax.shard_map(
        shards, mesh=mesh, in_specs=placed, out_specs=(P(("pair", "aux")), P()), check_vma=False
    )
```

```python
import itertools

import jax
import jax.numpy as jnp
from jax import lax
from jax.experimental import pallas as pl
from jax.experimental.pallas import tpu as pltpu
from jax.sharding import PartitionSpec as P

OB = 8
VB = 512
STEPS = 2
GROUP = 128
GROUPS = 32
HALF = GROUP // 2
WIDE = STEPS * GROUP
DEPTH = 768
TOP = 32764.0

MESH = pl.DeviceIdType.MESH
spin_scale = 1.3


def steps(*sizes):
    return [s for s in itertools.product(*map(range, sizes)) if any(s)]


OTHER_CORE = (0, 0, 0, 0, 1)
OTHER_HALF = (0, 0, 0, 1, 0)


def hops(s):
    return sum(min(a, n - a) for a, n in zip(s, (4, 4, 2, 2, 2)))


ALL_PEERS = sorted(steps(4, 4, 2, 2, 2), key=lambda s: -hops(s))
PEERS = sorted(set(steps(4, 1, 2, 1, 1) + steps(1, 4, 2, 1, 1) + [OTHER_CORE, OTHER_HALF]))


def encode(v, out):
    v = v.reshape(-1, 16, WIDE)
    n = v.shape[0]
    halves = [v[:, :, t * GROUP : (t + 1) * GROUP] for t in range(STEPS)]
    top = jnp.maximum(*[jnp.max(jnp.abs(a), axis=0) for a in halves])
    power = jnp.ceil(jnp.log2(jnp.maximum(top, 1e-30)))
    scale = jnp.exp2(-power) * TOP
    for t, a in enumerate(halves):
        q = jnp.round(a * scale[None]).astype(jnp.int32).astype(jnp.int16)
        out[t * n * 16 : (t + 1) * n * 16, :] = q.reshape(n * 16, GROUP)
    out[STEPS * n * 16 : STEPS * n * 16 + 16, :] = power.astype(jnp.int32).astype(jnp.int16)


def decode(ref):
    rows = (ref.shape[0] - 16) // STEPS
    n = rows // 16
    power = ref[STEPS * rows : STEPS * rows + 16, :].astype(jnp.int32).astype(jnp.float32)
    scale = (jnp.exp2(power) * (1.0 / TOP))[None]
    halves = []
    for t in range(STEPS):
        q = ref[t * rows : (t + 1) * rows, :].astype(jnp.int32).astype(jnp.float32)
        halves.append((q.reshape(n, 16, GROUP) * scale).reshape(rows, GROUP))
    return jnp.concatenate(halves, axis=1)


def coded(rows):
    return STEPS * rows + 16


def loop(n, body):
    def step(i, carry):
        body(i)
        return carry

    lax.fori_loop(0, n, step, 0)


def kernel(
    x_hbm, owners_in, occ_block_in, virt_block_in, occ_energy_in, virt_in,
    rows_out, total_out,
    owners, occ_block, virt_block, occ_energy, virt, xv, w, part, inverse, last, evec, ebuf,
    snd1, rcv1, snd2, rcv2,
    load_sem, small_sem, es, er, s1, r1, s2, r2, hello,
):
    aux = lax.axis_index("aux")
    pair = lax.axis_index("pair")
    z, x, y = aux // 8, (aux // 2) % 4, aux % 2
    hi, core = pair // 2, pair % 2

    zs = [((z + i) % 4) * 8 for i in range(4)]
    xs = [((x + i) % 4) * 2 for i in range(4)]
    ys = [y, 1 - y]
    his = [hi * 2, 2 - hi * 2]
    cores = [core, 1 - core]

    def device(step):
        dz, dx, dy, dh, dc = step
        at = zs[dz] if isinstance(dz, int) else ((z + dz) % 4) * 8
        at = at + (xs[dx] if isinstance(dx, int) else ((x + dx) % 4) * 2)
        return at + (ys[dy] if isinstance(dy, int) else (y + dy) % 2), his[dh] + cores[dc]

    small = []
    for i, (a, b) in enumerate(
        ((owners_in, owners), (occ_block_in, occ_block), (virt_block_in, virt_block),
         (occ_energy_in, occ_energy), (virt_in, virt))
    ):
        small.append(pltpu.make_async_copy(a, b, small_sem.at[i]))
    loads = []
    for i in range(4):
        rows = pl.ds(i * 8, 8)
        loads.append(pltpu.make_async_copy(x_hbm.at[rows], xv.at[rows], load_sem.at[i]))
    barrier = pltpu.get_barrier_semaphore()
    for c in loads + small:
        c.start()
    for s in PEERS:
        pl.semaphore_signal(barrier, inc=1, device_id=device(s), device_id_type=MESH)
    for c in small:
        c.wait()

    def gap_row(u):
        return virt[pl.ds(virt_block[pair] * 4 + u % 4, 1), :] - occ_energy[occ_block[pair] * 8 + u // 4]

    own_gap = jnp.transpose(jnp.broadcast_to(gap_row(aux), (GROUP, GROUP)))
    for t in range(STEPS):
        inverse[t] = 1.0 / (own_gap + gap_row(owners[t]))

    for c in loads:
        c.wait()
    for t in range(STEPS):
        w[t * GROUP : (t + 1) * GROUP, :] = xv[owners[t]].reshape(GROUP, DEPTH)

    def partial(h, k, dy):
        parts = []
        for j in range(4):
            dz, dx = j * (1 - h) + k * h, k * (1 - h) + j * h
            u = ((z + dz) % 4) * 8 + ((x + dx) % 4) * 2 + ((y + dy) % 2)
            parts.append(xv[u, h])
        rows = jnp.concatenate(parts, axis=0)
        v = lax.dot_general(rows, w[...], (((1,), (1,)), ((), ())), preferred_element_type=jnp.float32)
        part[h, k, dy] = v.reshape(2, 2, HALF, WIDE)

    def copy(src, dst, ssem, rsem, step):
        return pltpu.make_async_remote_copy(
            src_ref=src, dst_ref=dst, send_sem=ssem, recv_sem=rsem,
            device_id=device(step), device_id_type=MESH,
        )

    def post(dy, h, i, v, k):
        encode(v, snd1.at[dy, h, i])
        copy(
            snd1.at[dy, h, i], rcv1.at[dy, h, i], s1.at[dy, h, i], r1.at[dy, h, i],
            (k * h, k * (1 - h), 0, 0, 0),
        ).start()

    def take(dy, h, i):
        ref = rcv1.at[dy, h, i]
        pltpu.make_async_copy(ref, ref, r1.at[dy, h, i]).wait()
        return decode(ref)

    def side(h, k, dy, e):
        return part[h, k, dy, e].reshape(2 * HALF, WIDE)

    def far(dy, h, d):
        post(dy, h, d, side(h, 2, dy, d), 3 - 2 * d)

    def near(dy, h, d):
        post(dy, h, 2 + d, side(h, 1 + 2 * d, dy, d), 1 + 2 * d)

    def relay(dy, h, d):
        post(dy, h, 4 + d, side(h, 1 + 2 * d, dy, 1 - d) + take(dy, h, 1 - d), 1 + 2 * d)

    def gather(dy, h, e):
        v = side(h, 0, dy, e) + take(dy, h, 2 + e) + take(dy, h, 5 - e)
        part[h, 0, dy, e] = v.reshape(2, HALF, WIDE)

    def spread(dy, h, j):
        slot = j if dy else 3 + j
        encode(part[h, 0, dy, j // 2, j % 2], snd2.at[h, slot])
        copy(
            snd2.at[h, slot], rcv2.at[h, slot], s2.at[dy, h], r2.at[dy, h],
            (j * (1 - h), j * h, dy, 0, 0),
        ).start()

    def spread_wait(ref, sem, dy, h):
        here = ref.at[h, pl.ds(0, 4)] if dy else ref.at[h, pl.ds(4, 3)]
        pltpu.make_async_copy(here, here, sem.at[dy, h]).wait()

    def settle(h):
        spread_wait(rcv2, r2, 1, h)
        part[h, 0, 0, 0, 0] = part[h, 0, 0, 0, 0] + sum(decode(rcv2.at[h, i]) for i in range(4))

    def finish(h):
        spread_wait(rcv2, r2, 0, h)
        whole = part[h, 0, 0, 0, 0] + sum(decode(rcv2.at[h, i]) for i in range(4, 7))
        rows = pl.ds(h * HALF, HALF)
        terms = []
        for t in range(STEPS):
            v = whole[:, t * GROUP : (t + 1) * GROUP]
            terms.append(v * v * inverse[t, rows, :])
        last[rows, :] = terms[0] + terms[1]

    def close():
        def sent(i):
            dy, h, m = i // 12, (i // 6) % 2, i % 6
            ref = snd1.at[dy, h, m]
            pltpu.make_async_copy(ref, ref, s1.at[dy, h, m]).wait()

        loop(24, sent)
        for h in range(2):
            for dy in range(2):
                spread_wait(snd2, s2, dy, h)

    pairs = lambda f, dy: loop(4, lambda i: f(dy, i // 2, i % 2))

    def first(h):
        partial(h, 2, 1)
        loop(2, lambda d: far(1, h, d))

    def second(i):
        partial(i // 2, 1 + 2 * (i % 2), 1)
        near(1, i // 2, i % 2)

    def third(h):
        partial(h, 2, 0)
        loop(2, lambda d: far(0, h, d))

    partial(0, 2, 1)
    partial(1, 2, 1)
    pl.semaphore_wait(barrier, len(PEERS))
    pairs(far, 1)
    for k in range(1, 4):
        pl.semaphore_signal(hello.at[0], inc=1, device_id=device((0, k, 0, 0, 0)), device_id_type=MESH)
    loop(4, second)
    loop(2, third)
    pl.semaphore_wait(hello.at[0], 3)
    pl.semaphore_signal(hello.at[1], inc=1, device_id=device(OTHER_HALF), device_id_type=MESH)
    loop(4, lambda i: partial(i // 2, 1 + 2 * (i % 2), 0))
    pairs(relay, 1)
    pairs(near, 0)
    loop(4, lambda i: partial(i // 2, 0, i % 2))
    pairs(relay, 0)
    pl.semaphore_wait(hello.at[1], 1)
    pl.semaphore_signal(hello.at[2], inc=1, device_id=device(OTHER_CORE), device_id_type=MESH)
    for h in range(2):
        loop(2, lambda e: gather(1, h, e))
        loop(4, lambda i: spread(1, h, lax.rem(i + 2, 4)))
    for h in range(2):
        loop(2, lambda e: gather(0, h, e))
        loop(3, lambda i: spread(0, h, 1 + lax.rem(i + 1, 3)))
    for h in range(2):
        settle(h)
    for h in range(2):
        finish(h)
    pl.semaphore_wait(hello.at[2], 1)

    total = jnp.sum(last[...], axis=0, keepdims=True) * -spin_scale
    evec[...] = total
    for i, s in enumerate(ALL_PEERS):
        copy(evec, ebuf.at[i], es, er, s).start()
    rows_out[...] = jnp.sum(jnp.transpose(last[...]), axis=0, keepdims=True) * -spin_scale
    close()
    pltpu.make_async_copy(ebuf, ebuf, es).wait()
    pltpu.make_async_copy(ebuf, ebuf, er).wait()
    total_out[...] = total + jnp.sum(ebuf[...], axis=0)


def tail(rows, total, rows_out, mean_out):
    rows_out[...] = rows[...]
    mean_out[...] = jnp.sum(total[...], axis=1, keepdims=True) * (1.0 / (4 * GROUPS * GROUP))


def shards(ia_aux, occ_block, virt_block, owners, occ_energy, virt_energy):
    vmem = pl.BlockSpec(memory_space=pltpu.VMEM)
    dma = lambda *n: pltpu.SemaphoreType.DMA(n) if n else pltpu.SemaphoreType.DMA
    row = jax.ShapeDtypeStruct((1, GROUP), jnp.float32)
    row_energy, total = pl.pallas_call(
        kernel,
        out_shape=(pltpu.VMEM((1, GROUP), jnp.float32), pltpu.VMEM((1, GROUP), jnp.float32)),
        in_specs=[pl.BlockSpec(memory_space=pl.ANY)] * 6,
        out_specs=(vmem, vmem),
        scratch_shapes=[
            pltpu.SMEM((STEPS,), jnp.int32),
            pltpu.SMEM(occ_block.shape, jnp.int32),
            pltpu.SMEM(virt_block.shape, jnp.int32),
            pltpu.SMEM(occ_energy.shape, jnp.float32),
            pltpu.VMEM((virt_energy.shape[0] // GROUP, GROUP), jnp.float32),
            pltpu.VMEM((GROUPS, 2, HALF, DEPTH), jnp.bfloat16),
            pltpu.VMEM((WIDE, DEPTH), jnp.bfloat16),
            pltpu.VMEM((2, 4, 2, 2, 2, HALF, WIDE), jnp.float32),
            pltpu.VMEM((STEPS, GROUP, GROUP), jnp.float32),
            pltpu.VMEM((GROUP, GROUP), jnp.float32),
            pltpu.VMEM((1, GROUP), jnp.float32),
            pltpu.VMEM((len(ALL_PEERS), 1, GROUP), jnp.float32),
            pltpu.VMEM((2, 2, 6, coded(2 * HALF), GROUP), jnp.int16),
            pltpu.VMEM((2, 2, 6, coded(2 * HALF), GROUP), jnp.int16),
            pltpu.VMEM((2, 7, coded(HALF), GROUP), jnp.int16),
            pltpu.VMEM((2, 7, coded(HALF), GROUP), jnp.int16),
            dma(4), dma(5), dma(), dma(),
            dma(2, 2, 6), dma(2, 2, 6), dma(2, 2), dma(2, 2), pltpu.SemaphoreType.REGULAR((3,)),
        ],
        compiler_params=pltpu.CompilerParams(
            collective_id=0, has_side_effects=True, vmem_limit_bytes=56 * 2**20
        ),
    )(
        ia_aux.reshape(GROUPS, 2, HALF, DEPTH),
        owners,
        occ_block,
        virt_block,
        occ_energy,
        virt_energy.reshape(-1, GROUP),
    )
    row_energy, total = (pltpu.with_memory_space_constraint(a, pltpu.VMEM) for a in (row_energy, total))
    row_energy, mean = pl.pallas_call(
        tail, out_shape=(row, jax.ShapeDtypeStruct((1, 1), jnp.float32)), in_specs=[vmem, vmem]
    )(row_energy, total)
    return row_energy.reshape(GROUP), mean.reshape(())


def solution(mesh):
    placed = (P("pair", "aux"), P(), P(), P(), P(), P())
    return jax.shard_map(
        shards, mesh=mesh, in_specs=placed, out_specs=(P(("pair", "aux")), P()), check_vma=False
    )
```
